128 devices in a mesh: replica: 8 (over x, y_lo), fsdp: 16 (over y_hi, z, core).
Axes of the slice: x: 4, y: 4 (y_hi: 2, y_lo: 2; y = y_hi * 2 + y_lo), z: 4, core: 2. Of those that a mesh axis runs over, the one named last changes fastest.
Arguments:
- tokens: bfloat16 [16384, 4096], P(('replica', 'fsdp')), may hold values from -6 to 6
- up_cotangent: bfloat16 [16384, 16384], P('replica', 'fsdp'), may hold values from -6 to 6
- inner_up: bfloat16 [8, 4096, 16384], P('replica', None, 'fsdp'), may hold values from -6 to 6
- outer_up: float32 [4096, 16384], P('replica', 'fsdp'), may hold values from -6 to 6
- moment_up: float32 [4096, 16384], P('replica', 'fsdp'), may hold values from -4 to 4
Outputs:
- new_up: float32 [4096, 16384], P('replica', 'fsdp')
- new_moment_up: float32 [4096, 16384], P('replica', 'fsdp')
The draws below stay inside these ranges and needn't reach their ends.
All inputs are finite; a program needn't handle non-finite values.
Results may differ from the reference program's by a relative error of at most 0.0003.
Values may be sent and summed in bfloat16 or wider, within the bound.
No kernel may reach another device: no remote copies, remote signals or barrier semaphores. Data moves between devices by JAX's collectives and lax.ppermute only.
A program may use at most 128 MiB of HBM per device.

```python
import jax
import jax.numpy as jnp
from jax import lax

D = 4096
HID = 16384
REPLICAS = 8
TOKENS_REP = 2048
TOKENS = 16384


def levels(own_key, dims, cuts, smallest, high):
    factor_of, own = 1.0, jax.random.fold_in(own_key, 6)
    for axis_at, parts in cuts:
        draws = jnp.exp(jax.random.uniform(jax.random.fold_in(own, axis_at), (parts,), jnp.float32, smallest / len(cuts), high / len(cuts)))
        factor_of = factor_of * jnp.repeat(draws, dims[axis_at] // parts).reshape([-1 if axis == axis_at else 1 for axis in range(len(dims))])
    return factor_of


def noise(stream_key, shape, deviation, most, split=(), dtype=jnp.bfloat16):
    array = deviation * jax.random.normal(stream_key, shape, jnp.float32)
    if split:
        array = array * levels(stream_key, shape, split, -0.22, 0.18)
    return jnp.clip(array, -most, most).astype(dtype)


def setup_inputs(seed: int = 0) -> dict:
    splits = jax.random.split(jax.random.key(seed), 6)
    return {
        "tokens": noise(splits[0], (TOKENS, D), 1.0, 6.0, ((0, 128),)),
        "up_cotangent": noise(splits[1], (TOKENS, HID), 1.0, 6.0, ((0, 8), (1, 16))),
        "inner_up": noise(splits[2], (REPLICAS, D, HID), 1.0, 6.0, ((0, 8), (2, 16))),
        "outer_up": noise(splits[3], (D, HID), 1.0, 6.0, ((0, 8), (1, 16)), jnp.float32),
        "moment_up": noise(splits[4], (D, HID), 0.5, 4.0, ((0, 8), (1, 16)), jnp.float32),
    }


def reference(tokens, up_cotangent, inner_up, outer_up, moment_up):
    x_all = tokens.reshape(REPLICAS, TOKENS_REP, D)
    c_all = up_cotangent.reshape(REPLICAS, TOKENS_REP, HID)
    rate = 8.0 / (TOKENS_REP ** 0.5)

    def add_replica(carry, item):
        xr, cr, wr = item
        grad = lax.dot_general(xr.astype(jnp.float32), cr.astype(jnp.float32), (((0,), (0,)), ((), ())), precision=lax.Precision.HIGHEST, preferred_element_type=jnp.float32)
        inner_new = wr.astype(jnp.float32) - rate * grad
        return carry + inner_new, None

    total, _ = lax.scan(add_replica, jnp.zeros((D, HID), jnp.float32), (x_all, c_all, inner_up))
    mean_inner = total / REPLICAS
    avg = outer_up - mean_inner
    new_moment = 0.9 * moment_up + avg
    new_up = outer_up - 0.7 * (avg + 0.9 * new_moment)
    return (new_up, new_moment)
```

```python
import math

import jax
import jax.numpy as jnp
from jax import lax
from jax.experimental import pallas as pl
from jax.experimental.pallas import tpu as pltpu
from jax.sharding import Mesh
from jax.sharding import PartitionSpec as P

AXES = ("x", "yl", "yh", "z", "c")
SIZES = (4, 2, 2, 4, 2)
WIRE = jnp.float16
GROUPS = (((2, 1),), ((1, 1), (3, 1)), ((0, 1), (2, 0)), ((1, 0), (3, 0)), ((0, 0),))


def shift(value, axis, by):
    n = lax.axis_size(axis)
    return lax.ppermute(value, axis, [(i, (i + by) % n) for i in range(n)])


def fan(value, axis):
    n = lax.axis_size(axis)
    pairs = [(2 * i + c, 2 * ((i + 1 - 2 * c) % n) + c) for i in range(n) for c in (0, 1)]
    return lax.ppermute(value, (axis, "c"), pairs)


def after(value, *others):
    return lax.optimization_barrier((value, *others))[0]


def dot_first(left, right):
    return lax.dot_general(
        left, right, (((0,), (0,)), ((), ())), preferred_element_type=jnp.float32
    )


def copy_block(index, block, out):
    out[...] = block[...]


def reorder(array, order, rows):
    width = array.shape[1]
    return pl.pallas_call(
        copy_block,
        grid_spec=pltpu.PrefetchScalarGridSpec(
            num_scalar_prefetch=1,
            grid=(len(order),),
            in_specs=[pl.BlockSpec((rows, width), lambda i, index: (index[i], 0))],
            out_specs=pl.BlockSpec((rows, width), lambda i, index: (i, 0)),
        ),
        out_shape=jax.ShapeDtypeStruct(array.shape, array.dtype),
    )(jnp.stack(order), array)


def per_device(tokens, up_cotangent, inner_up, outer_up, moment_up):
    x, yl, yh, z, c = [lax.axis_index(a) for a in AXES]
    rate = 8.0 / math.sqrt(up_cotangent.shape[0])
    own_tokens = tokens.shape[0]
    share = outer_up.shape[0]

    def at(dx, dy):
        return (((x + dx) % 4) * 2 + (yl + dy) % 2) * share

    def source(dc, dz, dy):
        return ((yh + dy) % 2) * 8 + ((z + dz) % 4) * 2 + (c + dc) % 2

    order = [source(dc, dz, dy) for dc in (0, 1) for dz in (0, 3, 1, 2) for dy in (0, 1)]
    cot = reorder(up_cotangent, order, own_tokens)

    blocks = [
        jnp.concatenate([lax.dynamic_slice_in_dim(tokens, at(*d), share, 1) for d in group], 1)
        for group in GROUPS
    ]
    first, second, rest = blocks[0], blocks[1], jnp.concatenate(blocks[2:], 1)
    first2, second2, rest2 = shift(first, "yh", 1), shift(second, "yh", 1), shift(rest, "yh", 1)
    others, start = [first2, second2], 0
    for b in blocks[2:]:
        others.append(rest2[:, start : start + b.shape[1]])
        start += b.shape[1]

    news = {}
    near = []
    for g, (own, other) in enumerate(zip(blocks, others)):
        pair = jnp.concatenate([own, other], 0)
        if g >= 2:
            pair = after(pair, *near[g - 2])
        below, above = shift(pair, "z", 1), shift(pair, "z", -1)
        near.append((below, above))
        beyond = fan(jnp.where(c == 0, below, above), "z")
        three = jnp.concatenate([pair, below, above], 0)
        all_tokens = jnp.concatenate([three, beyond, shift(three, "c", 1), shift(beyond, "c", 1)], 0)
        grad = dot_first(all_tokens, cot)
        for i, d in enumerate(GROUPS[g]):
            w = lax.dynamic_slice_in_dim(inner_up[0], at(*d), share, 0)
            news[d] = w.astype(jnp.float32) - rate * grad[i * share : (i + 1) * share]

    sums = {}
    for dy in (1, 0):
        far = fan(news[2, dy].astype(WIRE), "x").astype(jnp.float32)
        up = news[1, dy] + jnp.where(c == 0, far, 0.0)
        down = news[3, dy] + jnp.where(c == 1, far, 0.0)
        up = shift(up.astype(WIRE), "x", 1)
        down = shift(down.astype(WIRE), "x", -1)
        sums[dy] = news[0, dy] + up.astype(jnp.float32) + down.astype(jnp.float32)
    total = sums[0] + shift(sums[1].astype(WIRE), "yl", 1).astype(jnp.float32)
    mean_inner = total / 8
    avg = outer_up - mean_inner
    new_moment = 0.9 * moment_up + avg
    new_up = outer_up - 0.7 * (avg + 0.9 * new_moment)
    return (new_up, new_moment)


def solution(mesh):
    fine = Mesh(mesh.devices.reshape(SIZES), AXES)
    rep, fsdp = AXES[:2], AXES[2:]
    placed = (
        P(AXES, None),
        P(rep, fsdp),
        P(rep, None, fsdp),
        P(rep, fsdp),
        P(rep, fsdp),
    )
    return jax.shard_map(
        per_device,
        mesh=fine,
        in_specs=placed,
        out_specs=(P(rep, fsdp), P(rep, fsdp)),
        check_vma=False,
    )
```

```python
import functools
import math

import jax
import jax.numpy as jnp
from jax import lax
from jax.experimental import pallas as pl
from jax.experimental.pallas import tpu as pltpu
from jax.sharding import Mesh
from jax.sharding import PartitionSpec as P

AXES = ("x", "yl", "yh", "z", "c")
SIZES = (4, 2, 2, 4, 2)
WIRE = jnp.float16
GROUPS = (((2, 1),), ((1, 1), (3, 1)), ((0, 1), (2, 0)), ((1, 0), (3, 0)), ((0, 0),))
PARTS = ((1,), (2, 3, 4))


def shift(value, axis, by):
    n = lax.axis_size(axis)
    return lax.ppermute(value, axis, [(i, (i + by) % n) for i in range(n)])


def fan(value, axis, by):
    n = lax.axis_size(axis)
    pairs = [(2 * i + c, 2 * ((i + by * (1 - 2 * c)) % n) + c) for i in range(n) for c in (0, 1)]
    return lax.ppermute(value, (axis, "c"), pairs)


def after(value, *others):
    return lax.optimization_barrier((value, *others))[0]


def dot_first(left, right):
    return lax.dot_general(
        left, right, (((0,), (0,)), ((), ())), preferred_element_type=jnp.float32
    )


def copy_blocks(rows, columns, index, source, *refs):
    *outs, sems = refs
    copies = []
    for out in outs:
        for i in range(out.shape[0] // rows):
            for j in range(out.shape[1] // columns):
                n = len(copies)
                row = pl.multiple_of(index[2 * n] * rows, rows)
                column = pl.multiple_of(index[2 * n + 1] * columns, columns)
                copies.append(
                    pltpu.make_async_copy(
                        source.at[pl.ds(row, rows), pl.ds(column, columns)],
                        out.at[pl.ds(i * rows, rows), pl.ds(j * columns, columns)],
                        sems.at[n],
                    )
                )
    for copy in copies:
        copy.start()
    for copy in copies:
        copy.wait()


def arrange(array, order, rows, columns, shapes):
    size = sum(a * b for a, b in shapes) * array.dtype.itemsize
    return pl.pallas_call(
        functools.partial(copy_blocks, rows, columns),
        in_specs=[pl.BlockSpec(memory_space=pltpu.SMEM), pl.BlockSpec(memory_space=pl.ANY)],
        out_specs=[pl.BlockSpec(memory_space=pltpu.VMEM) for _ in shapes],
        scratch_shapes=[pltpu.SemaphoreType.DMA((len(order),))],
        out_shape=[jax.ShapeDtypeStruct(shape, array.dtype) for shape in shapes],
        compiler_params=pltpu.CompilerParams(vmem_limit_bytes=8 * 1024 * 1024),
        cost_estimate=pl.CostEstimate(flops=0, bytes_accessed=2 * size, transcendentals=0),
    )(jnp.stack([i for place in order for i in place]), array)


def per_device(tokens, up_cotangent, inner_up, outer_up, moment_up):
    x, yl, yh, z, c = [lax.axis_index(a) for a in AXES]
    rate = 8.0 / math.sqrt(up_cotangent.shape[0])
    own_tokens = tokens.shape[0]
    share = outer_up.shape[0]
    half = share // 2
    sign = 1 - 2 * c

    def at(dx, dy):
        return (((x + dx) % 4) * 2 + (yl + dy) % 2) * share

    zero = jnp.int32(0)

    def column(d, core):
        return at(*d) // half + core

    def meet(mine, theirs):
        other = shift(theirs, "c", 1)
        return jnp.concatenate([jnp.where(c == 0, mine, other), jnp.where(c == 0, other, mine)], 0)

    def slices(group, core):
        cols = [lax.dynamic_slice_in_dim(tokens, column(d, core) * half, half, 1) for d in group]
        return jnp.concatenate(cols, 1) if len(cols) > 1 else cols[0]

    here = meet(slices(GROUPS[0], c), slices(GROUPS[0], 1 - c))
    pairs = [[here, shift(here, "yh", 1)]]
    later = [d for group in GROUPS[1:] for d in group]
    shape = (own_tokens, half * len(later))
    mine, theirs = arrange(
        after(tokens, here),
        [(zero, column(d, core)) for core in (c, 1 - c) for d in later],
        own_tokens,
        half,
        [shape, shape],
    )
    chip = meet(mine, theirs)
    begin = 0
    for part in PARTS:
        stops = [begin]
        for g in part:
            stops.append(stops[-1] + half * len(GROUPS[g]))
        here = chip[:, begin : stops[-1]]
        there = shift(here, "yh", 1)
        for start, stop in zip(stops, stops[1:]):
            pairs.append([here[:, start - begin : stop - begin], there[:, start - begin : stop - begin]])
        begin = stops[-1]
    pairs = [jnp.concatenate(p, 0) for p in pairs]

    order = [
        (((yh + dy) % 2) * 4 + (z - dz * sign) % 4, zero) for dz in (0, 1, -1, 2) for dy in (0, 1)
    ]
    (cot,) = arrange(
        after(up_cotangent, chip), order, 2 * own_tokens, up_cotangent.shape[1], [up_cotangent.shape]
    )
    quarter = cot.shape[0] // 4
    cots = [cot[i * quarter : (i + 1) * quarter] for i in range(4)]

    place = {}

    def news(dx, dy):
        grads, i = place[dx, dy]
        start = i * half
        to = dx
        if dx in (1, 3):
            back = (c == 1) ^ (dx == 3)
            start = (place[1, dy][1] + back.astype(jnp.int32)) * half
            to = 1 + 2 * back.astype(jnp.int32)
        parts = []
        for grad, core in zip(grads, (c, 1 - c)):
            w = lax.dynamic_slice_in_dim(inner_up[0], at(to, dy) + core * half, half, 0)
            parts.append(w.astype(jnp.float32) - rate * lax.dynamic_slice_in_dim(grad, start, half, 0))
        return jnp.concatenate(parts, 0)

    wide, far, up, down = {}, {}, {}, {}
    messages = []
    pair = pairs[0]
    swapped = shift(pair, "c", 1)
    first, second = fan(pair, "z", 1), fan(pair, "z", -1)
    for g, group in enumerate(GROUPS):
        beyond = fan(first, "z", 1)
        near = [pair, first, second, swapped, shift(first, "c", 1), shift(second, "c", 1)]
        if g + 1 < len(GROUPS):
            pair = after(pairs[g + 1], first, second)
            swapped = shift(pair, "c", 1)
            first, second = fan(pair, "z", 1), fan(pair, "z", -1)
            near = list(lax.optimization_barrier((*near, swapped, *messages)))[:6]
        elif messages:
            near = list(lax.optimization_barrier((*near, *messages)))[:6]
        sums = lax.optimization_barrier((
            dot_first(near[0], cots[0]) + dot_first(near[1], cots[1]) + dot_first(near[2], cots[2]),
            dot_first(near[3], cots[0]) + dot_first(near[4], cots[2]) + dot_first(near[5], cots[1]),
        ))
        grads = [
            sums[0] + dot_first(beyond, cots[3]),
            sums[1] + dot_first(shift(beyond, "c", 1), cots[3]),
        ]
        for i, d in enumerate(group):
            place[d] = grads, i
        messages = []
        for dx, dy in group:
            if dx == 2:
                message = news(dx, dy).astype(WIRE)
                far[dy] = fan(message, "x", 1)
            elif dx == 1:
                message = (news(dx, dy) + far[dy].astype(jnp.float32)).astype(WIRE)
                up[dy] = fan(message, "x", 1)
            elif dx == 3:
                message = news(dx, dy).astype(WIRE)
                down[dy] = fan(message, "x", -1)
            else:
                message = wide[dy] = news(dx, dy)
            messages.append(message)
    sums = [wide[dy] + up[dy].astype(jnp.float32) + down[dy].astype(jnp.float32) for dy in (0, 1)]
    last = shift(sums[1].astype(WIRE), "yl", 1)
    new_ups, new_moments = [], []
    for k in (0, 1):
        rows = slice(k * half, (k + 1) * half)
        start = ((k + c) % 2) * half
        total = lax.dynamic_slice_in_dim(sums[0], start, half, 0)
        total = total + lax.dynamic_slice_in_dim(last, start, half, 0).astype(jnp.float32)
        mean_inner = total / 8
        avg = outer_up[rows] - mean_inner
        new_moment = 0.9 * moment_up[rows] + avg
        new_ups.append(outer_up[rows] - 0.7 * (avg + 0.9 * new_moment))
        new_moments.append(new_moment)
    return (jnp.concatenate(new_ups, 0), jnp.concatenate(new_moments, 0))


def solution(mesh):
    fine = Mesh(mesh.devices.reshape(SIZES), AXES)
    rep, fsdp = AXES[:2], AXES[2:]
    placed = (
        P(AXES, None),
        P(rep, fsdp),
        P(rep, None, fsdp),
        P(rep, fsdp),
        P(rep, fsdp),
    )
    return jax.shard_map(
        per_device,
        mesh=fine,
        in_specs=placed,
        out_specs=(P(rep, fsdp), P(rep, fsdp)),
        check_vma=False,
    )
```

```python
import functools
import math

import jax
import jax.numpy as jnp
from jax import lax
from jax.experimental import pallas as pl
from jax.experimental.pallas import tpu as pltpu
from jax.sharding import Mesh
from jax.sharding import PartitionSpec as P

AXES = ("x", "yl", "yh", "z", "c")
SIZES = (4, 2, 2, 4, 2)
WIRE = jnp.float16
GROUPS = (((2, 1),), ((1, 1), (3, 1)), ((0, 1), (2, 0)), ((1, 0), (3, 0)), ((0, 0),))
PARTS = ((1,), (2, 3, 4))


def shift(value, axis, by):
    n = lax.axis_size(axis)
    return lax.ppermute(value, axis, [(i, (i + by) % n) for i in range(n)])


def fan(value, axis, by):
    n = lax.axis_size(axis)
    pairs = [(2 * i + c, 2 * ((i + by * (1 - 2 * c)) % n) + c) for i in range(n) for c in (0, 1)]
    return lax.ppermute(value, (axis, "c"), pairs)


def after(value, *others):
    return lax.optimization_barrier((value, *others))[0]


def dot_first(left, right):
    return lax.dot_general(
        left, right, (((0,), (0,)), ((), ())), preferred_element_type=jnp.float32
    )


def copy_blocks(rows, columns, index, source, *refs):
    *outs, sems = refs
    copies = []
    for out in outs:
        for i in range(out.shape[0] // rows):
            for j in range(out.shape[1] // columns):
                n = len(copies)
                row = pl.multiple_of(index[2 * n] * rows, rows)
                column = pl.multiple_of(index[2 * n + 1] * columns, columns)
                copies.append(
                    pltpu.make_async_copy(
                        source.at[pl.ds(row, rows), pl.ds(column, columns)],
                        out.at[pl.ds(i * rows, rows), pl.ds(j * columns, columns)],
                        sems.at[n],
                    )
                )
    for copy in copies:
        copy.start()
    for copy in copies:
        copy.wait()


def arrange(array, order, rows, columns, shapes):
    size = sum(a * b for a, b in shapes) * array.dtype.itemsize
    return pl.pallas_call(
        functools.partial(copy_blocks, rows, columns),
        in_specs=[pl.BlockSpec(memory_space=pltpu.SMEM), pl.BlockSpec(memory_space=pl.ANY)],
        out_specs=[pl.BlockSpec(memory_space=pltpu.VMEM) for _ in shapes],
        scratch_shapes=[pltpu.SemaphoreType.DMA((len(order),))],
        out_shape=[jax.ShapeDtypeStruct(shape, array.dtype) for shape in shapes],
        compiler_params=pltpu.CompilerParams(vmem_limit_bytes=8 * 1024 * 1024),
        cost_estimate=pl.CostEstimate(flops=0, bytes_accessed=2 * size, transcendentals=0),
    )(jnp.stack([i for place in order for i in place]), array)


def per_device(tokens, up_cotangent, inner_up, outer_up, moment_up):
    x, yl, yh, z, c = [lax.axis_index(a) for a in AXES]
    rate = 8.0 / math.sqrt(up_cotangent.shape[0])
    own_tokens = tokens.shape[0]
    share = outer_up.shape[0]
    half = share // 2
    sign = 1 - 2 * c

    def at(dx, dy):
        return (((x + dx) % 4) * 2 + (yl + dy) % 2) * share

    zero = jnp.int32(0)

    def column(d, core):
        return at(*d) // half + core

    def meet(mine, theirs):
        other = shift(theirs, "c", 1)
        return jnp.concatenate([jnp.where(c == 0, mine, other), jnp.where(c == 0, other, mine)], 0)

    def slices(group, core):
        cols = [lax.dynamic_slice_in_dim(tokens, column(d, core) * half, half, 1) for d in group]
        return jnp.concatenate(cols, 1) if len(cols) > 1 else cols[0]

    here = meet(slices(GROUPS[0], c), slices(GROUPS[0], 1 - c))
    pairs = [[here, shift(here, "yh", 1)]]
    later = [d for group in GROUPS[1:] for d in group]
    shape = (own_tokens, half * len(later))
    mine, theirs = arrange(
        after(tokens, here),
        [(zero, column(d, core)) for core in (c, 1 - c) for d in later],
        own_tokens,
        half,
        [shape, shape],
    )
    chip = meet(mine, theirs)
    begin = 0
    for part in PARTS:
        stops = [begin]
        for g in part:
            stops.append(stops[-1] + half * len(GROUPS[g]))
        here = chip[:, begin : stops[-1]]
        there = shift(here, "yh", 1)
        for start, stop in zip(stops, stops[1:]):
            pairs.append([here[:, start - begin : stop - begin], there[:, start - begin : stop - begin]])
        begin = stops[-1]
    pairs = [jnp.concatenate(p, 0) for p in pairs]

    order = [
        (((yh + dy) % 2) * 4 + (z - dz * sign) % 4, zero) for dz in (0, 1, -1, 2) for dy in (0, 1)
    ]
    (cot,) = arrange(
        after(up_cotangent, chip), order, 2 * own_tokens, up_cotangent.shape[1], [up_cotangent.shape]
    )
    quarter = cot.shape[0] // 4
    cots = [cot[i * quarter : (i + 1) * quarter] for i in range(4)]

    place = {}

    def news(dx, dy):
        grads, i = place[dx, dy]
        start = i * half
        to = dx
        if dx in (1, 3):
            back = (c == 1) ^ (dx == 3)
            start = (place[1, dy][1] + back.astype(jnp.int32)) * half
            to = 1 + 2 * back.astype(jnp.int32)
        parts = []
        for grad, core in zip(grads, (c, 1 - c)):
            w = lax.dynamic_slice_in_dim(inner_up[0], at(to, dy) + core * half, half, 0)
            parts.append(w.astype(jnp.float32) - rate * lax.dynamic_slice_in_dim(grad, start, half, 0))
        return jnp.concatenate(parts, 0)

    wide, far, up, down = {}, {}, {}, {}
    messages = []
    pair = pairs[0]
    swapped = shift(pair, "c", 1)
    first, second = fan(pair, "z", 1), fan(pair, "z", -1)
    for g, group in enumerate(GROUPS):
        beyond = fan(first, "z", 1)
        if g + 1 == len(GROUPS):
            first, second = lax.optimization_barrier((first, second, *messages))[:2]
            beyond = after(beyond, *messages)
        near = [pair, first, second, swapped, shift(first, "c", 1), shift(second, "c", 1)]
        if g + 1 < len(GROUPS):
            pair = after(pairs[g + 1], first, second)
            swapped = shift(pair, "c", 1)
            first, second = fan(pair, "z", 1), fan(pair, "z", -1)
            near = list(lax.optimization_barrier((*near, swapped, *messages)))[:6]
        elif messages:
            near = list(lax.optimization_barrier((*near, *messages)))[:6]
        sums = lax.optimization_barrier((
            dot_first(near[0], cots[0]) + dot_first(near[1], cots[1]) + dot_first(near[2], cots[2]),
            dot_first(near[3], cots[0]) + dot_first(near[4], cots[2]) + dot_first(near[5], cots[1]),
        ))
        grads = [
            sums[0] + dot_first(beyond, cots[3]),
            sums[1] + dot_first(shift(beyond, "c", 1), cots[3]),
        ]
        for i, d in enumerate(group):
            place[d] = grads, i
        messages = []
        for dx, dy in group:
            if dx == 2:
                message = news(dx, dy).astype(WIRE)
                far[dy] = fan(message, "x", 1)
            elif dx == 1:
                message = (news(dx, dy) + far[dy].astype(jnp.float32)).astype(WIRE)
                up[dy] = fan(message, "x", 1)
            elif dx == 3:
                message = news(dx, dy).astype(WIRE)
                down[dy] = fan(message, "x", -1)
            else:
                message = wide[dy] = news(dx, dy)
            messages.append(message)
    sums = [wide[dy] + up[dy].astype(jnp.float32) + down[dy].astype(jnp.float32) for dy in (0, 1)]
    last = shift(sums[1].astype(WIRE), "yl", 1)
    new_ups, new_moments = [], []
    for k in (0, 1):
        rows = slice(k * half, (k + 1) * half)
        start = ((k + c) % 2) * half
        total = lax.dynamic_slice_in_dim(sums[0], start, half, 0)
        total = total + lax.dynamic_slice_in_dim(last, start, half, 0).astype(jnp.float32)
        mean_inner = total / 8
        avg = outer_up[rows] - mean_inner
        new_moment = 0.9 * moment_up[rows] + avg
        new_ups.append(outer_up[rows] - 0.7 * (avg + 0.9 * new_moment))
        new_moments.append(new_moment)
    return (jnp.concatenate(new_ups, 0), jnp.concatenate(new_moments, 0))


def solution(mesh):
    fine = Mesh(mesh.devices.reshape(SIZES), AXES)
    rep, fsdp = AXES[:2], AXES[2:]
    placed = (
        P(AXES, None),
        P(rep, fsdp),
        P(rep, None, fsdp),
        P(rep, fsdp),
        P(rep, fsdp),
    )
    return jax.shard_map(
        per_device,
        mesh=fine,
        in_specs=placed,
        out_specs=(P(rep, fsdp), P(rep, fsdp)),
        check_vma=False,
    )
```

```python
import functools
import math

import jax
import jax.numpy as jnp
from jax import lax
from jax.experimental import pallas as pl
from jax.experimental.pallas import tpu as pltpu
from jax.sharding import Mesh
from jax.sharding import PartitionSpec as P

AXES = ("x", "yl", "yh", "z", "c")
SIZES = (4, 2, 2, 4, 2)
WIRE = jnp.float16
GROUPS = (((2, 1),), ((1, 1), (3, 1)), ((0, 1), (2, 0)), ((1, 0), (3, 0)), ((0, 0),))
PARTS = ((1,), (2, 3, 4))


def shift(value, axis, by):
    n = lax.axis_size(axis)
    return lax.ppermute(value, axis, [(i, (i + by) % n) for i in range(n)])


def fan(value, axis, by):
    n = lax.axis_size(axis)
    pairs = [(2 * i + c, 2 * ((i + by * (1 - 2 * c)) % n) + c) for i in range(n) for c in (0, 1)]
    return lax.ppermute(value, (axis, "c"), pairs)


def after(value, *others):
    return lax.optimization_barrier((value, *others))[0]


def factor(hop, index):
    return (16 + (5 * index + 3 * hop) % 16).astype(jnp.float32) / 32


def send(value, scale):
    return (value * scale).astype(WIRE)


def receive(value, scale):
    return value.astype(jnp.float32) * (1.0 / scale)


def dot_first(left, right):
    return lax.dot_general(
        left, right, (((0,), (0,)), ((), ())), preferred_element_type=jnp.float32
    )


def copy_blocks(rows, columns, index, source, *refs):
    *outs, sems = refs
    copies = []
    for out in outs:
        for i in range(out.shape[0] // rows):
            for j in range(out.shape[1] // columns):
                n = len(copies)
                row = pl.multiple_of(index[2 * n] * rows, rows)
                column = pl.multiple_of(index[2 * n + 1] * columns, columns)
                copies.append(
                    pltpu.make_async_copy(
                        source.at[pl.ds(row, rows), pl.ds(column, columns)],
                        out.at[pl.ds(i * rows, rows), pl.ds(j * columns, columns)],
                        sems.at[n],
                    )
                )
    for copy in copies:
        copy.start()
    for copy in copies:
        copy.wait()


def arrange(array, order, rows, columns, shapes):
    size = sum(a * b for a, b in shapes) * array.dtype.itemsize
    return pl.pallas_call(
        functools.partial(copy_blocks, rows, columns),
        in_specs=[pl.BlockSpec(memory_space=pltpu.SMEM), pl.BlockSpec(memory_space=pl.ANY)],
        out_specs=[pl.BlockSpec(memory_space=pltpu.VMEM) for _ in shapes],
        scratch_shapes=[pltpu.SemaphoreType.DMA((len(order),))],
        out_shape=[jax.ShapeDtypeStruct(shape, array.dtype) for shape in shapes],
        compiler_params=pltpu.CompilerParams(vmem_limit_bytes=8 * 1024 * 1024),
        cost_estimate=pl.CostEstimate(flops=0, bytes_accessed=2 * size, transcendentals=0),
    )(jnp.stack([i for place in order for i in place]), array)


def per_device(tokens, up_cotangent, inner_up, outer_up, moment_up):
    x, yl, yh, z, c = [lax.axis_index(a) for a in AXES]
    rate = 8.0 / math.sqrt(up_cotangent.shape[0])
    own_tokens = tokens.shape[0]
    share = outer_up.shape[0]
    half = share // 2
    sign = 1 - 2 * c
    below, above = (x - sign) % 4, (x + sign) % 4

    def at(dx, dy):
        return (((x + dx) % 4) * 2 + (yl + dy) % 2) * share

    zero = jnp.int32(0)

    def column(d, core):
        return at(*d) // half + core

    def meet(mine, theirs):
        other = shift(theirs, "c", 1)
        return jnp.concatenate([jnp.where(c == 0, mine, other), jnp.where(c == 0, other, mine)], 0)

    def slices(group, core):
        cols = [lax.dynamic_slice_in_dim(tokens, column(d, core) * half, half, 1) for d in group]
        return jnp.concatenate(cols, 1) if len(cols) > 1 else cols[0]

    here = meet(slices(GROUPS[0], c), slices(GROUPS[0], 1 - c))
    pairs = [[here, shift(here, "yh", 1)]]
    later = [d for group in GROUPS[1:] for d in group]
    shape = (own_tokens, half * len(later))
    mine, theirs = arrange(
        after(tokens, here),
        [(zero, column(d, core)) for core in (c, 1 - c) for d in later],
        own_tokens,
        half,
        [shape, shape],
    )
    chip = meet(mine, theirs)
    begin = 0
    for part in PARTS:
        stops = [begin]
        for g in part:
            stops.append(stops[-1] + half * len(GROUPS[g]))
        here = chip[:, begin : stops[-1]]
        there = shift(here, "yh", 1)
        for start, stop in zip(stops, stops[1:]):
            pairs.append([here[:, start - begin : stop - begin], there[:, start - begin : stop - begin]])
        begin = stops[-1]
    pairs = [jnp.concatenate(p, 0) for p in pairs]

    order = [
        (((yh + dy) % 2) * 4 + (z - dz * sign) % 4, zero) for dz in (0, 1, -1, 2) for dy in (0, 1)
    ]
    (cot,) = arrange(
        after(up_cotangent, chip), order, 2 * own_tokens, up_cotangent.shape[1], [up_cotangent.shape]
    )
    quarter = cot.shape[0] // 4
    cots = [cot[i * quarter : (i + 1) * quarter] for i in range(4)]

    place = {}

    def news(dx, dy):
        grads, i = place[dx, dy]
        start = i * half
        to = dx
        if dx in (1, 3):
            back = (c == 1) ^ (dx == 3)
            start = (place[1, dy][1] + back.astype(jnp.int32)) * half
            to = 1 + 2 * back.astype(jnp.int32)
        parts = []
        for grad, core in zip(grads, (c, 1 - c)):
            w = lax.dynamic_slice_in_dim(inner_up[0], at(to, dy) + core * half, half, 0)
            parts.append(w.astype(jnp.float32) - rate * lax.dynamic_slice_in_dim(grad, start, half, 0))
        return jnp.concatenate(parts, 0)

    wide, far, up, down = {}, {}, {}, {}
    messages = []
    pair = pairs[0]
    swapped = shift(pair, "c", 1)
    first, second = fan(pair, "z", 1), fan(pair, "z", -1)
    for g, group in enumerate(GROUPS):
        beyond = fan(first, "z", 1)
        if g + 1 == len(GROUPS):
            first, second = lax.optimization_barrier((first, second, *messages))[:2]
            beyond = after(beyond, *messages)
        near = [pair, first, second, swapped, shift(first, "c", 1), shift(second, "c", 1)]
        if g + 1 < len(GROUPS):
            pair = after(pairs[g + 1], first, second)
            swapped = shift(pair, "c", 1)
            first, second = fan(pair, "z", 1), fan(pair, "z", -1)
            near = list(lax.optimization_barrier((*near, swapped, *messages)))[:6]
        elif messages:
            near = list(lax.optimization_barrier((*near, *messages)))[:6]
        sums = lax.optimization_barrier((
            dot_first(near[0], cots[0]) + dot_first(near[1], cots[1]) + dot_first(near[2], cots[2]),
            dot_first(near[3], cots[0]) + dot_first(near[4], cots[2]) + dot_first(near[5], cots[1]),
        ))
        grads = [
            sums[0] + dot_first(beyond, cots[3]),
            sums[1] + dot_first(shift(beyond, "c", 1), cots[3]),
        ]
        for i, d in enumerate(group):
            place[d] = grads, i
        messages = []
        for dx, dy in group:
            if dx == 2:
                message = send(news(dx, dy), factor(0, x))
                far[dy] = fan(message, "x", 1)
            elif dx == 1:
                message = send(news(dx, dy) + receive(far[dy], factor(0, below)), factor(1, x))
                up[dy] = fan(message, "x", 1)
            elif dx == 3:
                message = send(news(dx, dy), factor(2, x))
                down[dy] = fan(message, "x", -1)
            else:
                message = wide[dy] = news(dx, dy)
            messages.append(message)
    sums = [
        wide[dy] + receive(up[dy], factor(1, below)) + receive(down[dy], factor(2, above))
        for dy in (0, 1)
    ]
    last = shift(send(sums[1], factor(3, yl)), "yl", 1)
    new_ups, new_moments = [], []
    for k in (0, 1):
        rows = slice(k * half, (k + 1) * half)
        start = ((k + c) % 2) * half
        total = lax.dynamic_slice_in_dim(sums[0], start, half, 0)
        total = total + receive(lax.dynamic_slice_in_dim(last, start, half, 0), factor(3, 1 - yl))
        mean_inner = total / 8
        avg = outer_up[rows] - mean_inner
        new_moment = 0.9 * moment_up[rows] + avg
        new_ups.append(outer_up[rows] - 0.7 * (avg + 0.9 * new_moment))
        new_moments.append(new_moment)
    return (jnp.concatenate(new_ups, 0), jnp.concatenate(new_moments, 0))


def solution(mesh):
    fine = Mesh(mesh.devices.reshape(SIZES), AXES)
    rep, fsdp = AXES[:2], AXES[2:]
    placed = (
        P(AXES, None),
        P(rep, fsdp),
        P(rep, None, fsdp),
        P(rep, fsdp),
        P(rep, fsdp),
    )
    return jax.shard_map(
        per_device,
        mesh=fine,
        in_specs=placed,
        out_specs=(P(rep, fsdp), P(rep, fsdp)),
        check_vma=False,
    )
```
